128 devices in a mesh: cell: 8 (over z, core), gene: 4 (over y), rank: 4 (over x).
Axes of the slice: x: 4, y: 4, z: 4, core: 2. Of those that a mesh axis runs over, the one named last changes fastest.
Arguments:
- blocks: bfloat16 [8, 16, 96, 256, 128], P('cell', ('gene', 'rank')), may hold values from -6 to 6
- block_pos: int32 [8, 16, 96], P('cell', ('gene', 'rank')), may hold values from 0 to 127, as said below
- block_count: int32 [8, 16], P('cell', ('gene', 'rank')), may hold values from 32 to 96, as said below
- test_right: bfloat16 [32768, 512], P(('gene', 'rank')), may hold values from -0.0625 to 0.0625
- test_left: bfloat16 [16384, 768], P('cell', 'rank'), may hold values from -0.09375 to 0.09375
- gene_sketch_old: float32 [768, 32768], P('cell', ('gene', 'rank')), may hold values from -4 to 4
Outputs:
- right_sketch: float32 [16384, 512], P(('cell', 'gene', 'rank'))
- gene_sketch: float32 [768, 32768], P('cell', ('gene', 'rank'))
- core: float32 [768, 512], P('cell')
The draws below stay inside these ranges and needn't reach their ends.
Inputs may be any that keep to these rules, and one draw needn't show every extreme that they name: `block_pos`: position p names row block p // 16 and gene block p % 16 of the device's tile; the 96 positions of one device are distinct. `block_count`: some device has all 96 slots live in every draw; slots from the count on are not part of A.
All inputs are finite; a program needn't handle non-finite values.
Results may differ from the reference program's by a relative error of at most 0.0003.
Values may be sent and summed in bfloat16 or wider, within the bound.
No kernel may reach another device: no remote copies, remote signals or barrier semaphores. Data moves between devices by JAX's collectives and lax.ppermute only.
A program may use at most 128 MiB of HBM per device.

```python
import jax
import jax.numpy as jnp
from jax import lax

BROWS = 256
BCOLS = 128
R = 512
L = 768
GB_DEV = 16
RB_DEV = 8
NB = 96
CSHARDS = 8
GSHARDS = 16
CELLS = 16384
GENES = 32768
N_CELL = 8
N_GENE = 4
N_RANK = 4


def draw_block_pos(key, part):
    devices = CSHARDS * GSHARDS
    tile_size = RB_DEV * GB_DEV
    subkeys = jax.random.split(key, devices)
    orders = jax.vmap(lambda single: jax.random.permutation(single, tile_size))(subkeys)
    return orders[:, :NB].reshape(CSHARDS, GSHARDS, NB).astype(jnp.int32)


def draw_block_count(key, part):
    first_key, second_key = jax.random.split(jax.random.fold_in(key, 7))
    devices = CSHARDS * GSHARDS
    spread = jax.random.randint(first_key, (devices,), 0, 65)
    floor_count = NB // 3
    counts = floor_count + (NB - floor_count) * spread * spread // 4096
    chosen = jax.random.randint(second_key, (), 0, devices)
    counts = jnp.where(jnp.arange(devices) == chosen, NB, counts)
    return counts.reshape(CSHARDS, GSHARDS).astype(jnp.int32)


def block_scale(stream_key, extent, cuts, least, high):
    gain = 1.0
    for dim, shards_of in cuts:
        heights = jax.random.uniform(jax.random.fold_in(jax.random.fold_in(stream_key, 6), dim), (shards_of,), jnp.float32, least / len(cuts), high / len(cuts))
        gain = gain * jnp.repeat(jnp.exp(heights), extent[dim] // shards_of).reshape((-1,) + (1,) * (len(extent) - 1 - dim))
    return gain


def scatter_about(stream_key, extent, deviation, bound, pieces=(), kind=jnp.bfloat16):
    loudness = block_scale(stream_key, extent, pieces, -0.22, 0.18) if pieces else 1.0
    values = jax.random.normal(stream_key, extent, jnp.float32) * deviation * loudness
    return jnp.minimum(jnp.maximum(values, -bound), bound).astype(kind)


def setup_inputs(seed: int = 0) -> dict:
    key_list = jax.random.split(jax.random.key(seed), 7)
    return {
        "blocks": scatter_about(key_list[0], (N_CELL, N_GENE * N_RANK, NB, BROWS, BCOLS), 1.0, 6.0, ((0, 8), (1, 16))),
        "block_pos": draw_block_pos(jax.random.fold_in(key_list[6], 71), 0),
        "block_count": draw_block_count(jax.random.fold_in(key_list[6], 71), 0),
        "test_right": scatter_about(key_list[3], (GENES, R), (GENES // 4) ** -0.5, 0.0625, ((0, 16),)),
        "test_left": scatter_about(key_list[4], (CELLS, L), (CELLS // 4) ** -0.5, 0.09375, ((0, 8), (1, 4))),
        "gene_sketch_old": scatter_about(key_list[5], (L, GENES), 0.5, 4.0, ((0, 8), (1, 16)), jnp.float32),
    }


def reference(blocks, block_pos, block_count, test_right, test_left, gene_sketch_old):
    highest = lax.Precision.HIGHEST
    cell_rows = RB_DEV * BROWS
    gene_cols = GB_DEV * BCOLS
    right_table = test_right.reshape(GSHARDS * GB_DEV, BCOLS, R)
    left_table = test_left.reshape(CSHARDS * RB_DEV, BROWS, L)
    slot_ids = jnp.arange(NB, dtype=jnp.int32)
    row_ids = jnp.arange(RB_DEV, dtype=jnp.int32)
    gene_ids = jnp.arange(GB_DEV, dtype=jnp.int32)

    def visit(carry, flat_index):
        right_acc, gene_acc = carry
        cell_index = flat_index // GSHARDS
        gene_index = flat_index % GSHARDS
        tiles = blocks[cell_index, gene_index].astype(jnp.float32)
        positions = block_pos[cell_index, gene_index]
        alive_mask = (slot_ids < block_count[cell_index, gene_index]).astype(jnp.float32)
        row_block = positions // GB_DEV
        gene_block = positions % GB_DEV
        right_rows = right_table[gene_index * GB_DEV + gene_block].astype(jnp.float32)
        left_rows = left_table[cell_index * RB_DEV + row_block].astype(jnp.float32)
        right_terms = jnp.einsum("pik,pkr->pir", tiles, right_rows, precision=highest) * alive_mask[:, None, None]
        gene_terms = jnp.einsum("pil,pik->plk", left_rows, tiles, precision=highest) * alive_mask[:, None, None]
        row_hot = (row_block[None, :] == row_ids[:, None]).astype(jnp.float32)
        gene_hot = (gene_block[None, :] == gene_ids[:, None]).astype(jnp.float32)
        right_tile = jnp.einsum("rp,pik->rik", row_hot, right_terms, precision=highest).reshape(cell_rows, R)
        gene_tile = jnp.einsum("gp,plk->lgk", gene_hot, gene_terms, precision=highest).reshape(L, gene_cols)
        row_start = (cell_index * cell_rows).astype(jnp.int32)
        col_start = (gene_index * gene_cols).astype(jnp.int32)
        anchor = jnp.zeros((), jnp.int32)
        old_rows = lax.dynamic_slice(right_acc, (row_start, anchor), (cell_rows, R))
        right_acc = lax.dynamic_update_slice(right_acc, old_rows + right_tile, (row_start, anchor))
        old_cols = lax.dynamic_slice(gene_acc, (anchor, col_start), (L, gene_cols))
        gene_acc = lax.dynamic_update_slice(gene_acc, old_cols + gene_tile, (anchor, col_start))
        return (right_acc, gene_acc), None

    initial = (jnp.zeros((CSHARDS * cell_rows, R), jnp.float32), jnp.zeros((L, GSHARDS * gene_cols), jnp.float32))
    (right_sketch, gene_sum), unused = lax.scan(visit, initial, jnp.arange(CSHARDS * GSHARDS, dtype=jnp.int32))
    core = lax.dot_general(test_left.astype(jnp.float32), right_sketch, (((0,), (0,)), ((), ())), precision=highest)
    return right_sketch, gene_sketch_old + gene_sum, core
```

```python
import functools

import jax
import jax.numpy as jnp
from jax import lax
from jax.experimental import pallas as pl
from jax.experimental.pallas import tpu as pltpu
from jax.sharding import PartitionSpec as P

ROWS = 2048
COLS = 2048
BR, BC = 256, 128
NB = 96
R = 512
HALF = 96
SPAN = 512
LIMIT = 24 * 1024 * 1024
F32 = jnp.float32
BF16 = jnp.bfloat16
I16 = jnp.int16
ANY = pl.BlockSpec(memory_space=pl.ANY)
HBM = pl.BlockSpec(memory_space=pltpu.HBM)
VMEM = pl.BlockSpec(memory_space=pltpu.VMEM)
SMEM = pl.BlockSpec(memory_space=pltpu.SMEM)


def params(**kw):
    return pltpu.CompilerParams(vmem_limit_bytes=LIMIT, **kw)


def cost(flops=1):
    return pl.CostEstimate(flops=flops, bytes_accessed=1, transcendentals=0)


def encode(x):
    rows, cols = x.shape
    lane = lax.broadcasted_iota(jnp.int32, (rows, 128), 1)
    codes = jnp.zeros((rows, 128), jnp.int32)
    parts = []
    for j in range(cols // SPAN):
        part = x[:, j * SPAN : (j + 1) * SPAN]
        top = jnp.max(jnp.abs(part), axis=1, keepdims=True)
        code = jnp.ceil(jnp.log2(jnp.maximum(top, 1e-30) * (1.0 / 32760.0)) * 256.0)
        inverse = jnp.exp2(code * (-1.0 / 256.0))
        parts.append(jnp.round(part * inverse).astype(jnp.int32).astype(I16))
        codes = jnp.where(lane == j, code.astype(jnp.int32), codes)
    return jnp.concatenate(parts + [codes.astype(I16)], axis=1)


def encode_part(part, out, j):
    rows = part.shape[0]
    end = out.shape[1] - 128
    lane = lax.broadcasted_iota(jnp.int32, (rows, 128), 1)
    coded = encode(part)
    out[:, j * SPAN : (j + 1) * SPAN] = coded[:, :SPAN]
    codes = coded[:, SPAN:].astype(jnp.int32)
    if j == 0:
        out[:, end:] = codes.astype(I16)
    else:
        moved = jnp.where(lane == j, codes[:, 0:1], out[:, end:].astype(jnp.int32))
        out[:, end:] = moved.astype(I16)


def decode(q):
    rows, cols = q.shape
    cols -= 128
    scales = jnp.exp2(q[:, cols:].astype(jnp.int32).astype(F32) * (1.0 / 256.0))
    parts = []
    for j in range(cols // SPAN):
        parts.append(q[:, j * SPAN : (j + 1) * SPAN].astype(jnp.int32).astype(F32) * scales[:, j : j + 1])
    return jnp.concatenate(parts, axis=1)


def first_kernel(pos, cnt, place, blocks, left_test, right_test, tile, right_out, far_low, far_high, mine, other, rt, left, right, rows, sems, io):
    live = cnt[0]
    get_rt = pltpu.make_async_copy(right_test, rt, io.at[0])
    get_rt.start()
    get_left = pltpu.make_async_copy(left_test, left, io.at[1 + ROWS // BR])
    get_left.start()

    def clear(i, _):
        tile[pl.ds(pl.multiple_of(i * 64, 64), 64), :] = jnp.zeros((64, COLS), BF16)

    lax.fori_loop(0, ROWS // 64, clear, None)

    def copy_of(s):
        p = pos[s]
        row = pl.multiple_of((p >> 4) * BR, BR)
        col = pl.multiple_of((p & 15) * BC, BC)
        return pltpu.make_async_copy(blocks.at[s], tile.at[pl.ds(row, BR), pl.ds(col, BC)], sems.at[s])

    lax.fori_loop(0, live, lambda s, _: copy_of(s).start(), None)
    get_left.wait()
    order_rows(place, [left.at[0:HALF], left.at[HALF : 2 * HALF]], rows)
    get_rt.wait()
    lax.fori_loop(0, live, lambda s, _: copy_of(s).wait(), None)

    def put_of(i):
        rows = pl.ds(pl.multiple_of(i * BR, BR), BR)
        return pltpu.make_async_copy(right.at[rows, :], right_out.at[rows, :], io.at[1 + i])

    def multiply(i, _):
        rows = pl.ds(pl.multiple_of(i * BR, BR), BR)
        right[rows, :] = jnp.dot(tile[rows, :], rt[...], preferred_element_type=F32)
        put_of(i).start()

    lax.fori_loop(0, ROWS // BR, multiply, None)
    far = pl.multiple_of(((place[1] + 2) & 3) * 2 * BR, 2 * BR)
    far_low[...] = encode(right[pl.ds(far, BR), :])
    far_high[...] = encode(right[pl.ds(far + BR, BR), :])
    for j in range(COLS // SPAN):
        cols = slice(j * SPAN, (j + 1) * SPAN)
        acc = jnp.dot(rows[...], tile[:, cols], preferred_element_type=F32)
        mine[0, :, cols] = acc[:HALF]
        encode_part(acc[HALF:], other, j)
    lax.fori_loop(0, ROWS // BR, lambda i, _: put_of(i).wait(), None)


def order_rows(place, halves, rows):
    for c in range(len(halves) // 2):
        low, high = halves[2 * c], halves[2 * c + 1]
        at = 2 * HALF * c

        @pl.when(place[0] == 0)
        def _():
            rows[at : at + HALF, :] = low[...]
            rows[at + HALF : at + 2 * HALF, :] = high[...]

        @pl.when(place[0] == 1)
        def _():
            rows[at : at + HALF, :] = high[...]
            rows[at + HALF : at + 2 * HALF, :] = low[...]


def first(pos, cnt, place, blocks, left, right_test):
    return pl.pallas_call(
        first_kernel,
        out_shape=[
            pltpu.VMEM((ROWS, COLS), BF16),
            jax.ShapeDtypeStruct((ROWS, R), F32),
            jax.ShapeDtypeStruct((BR, R + 128), I16),
            jax.ShapeDtypeStruct((BR, R + 128), I16),
            pltpu.VMEM((1, HALF, COLS), F32),
            jax.ShapeDtypeStruct((HALF, COLS + 128), I16),
        ],
        in_specs=[SMEM, SMEM, SMEM, HBM, HBM, HBM],
        out_specs=[VMEM, HBM, VMEM, VMEM, VMEM, VMEM],
        scratch_shapes=[
            pltpu.VMEM((COLS, R), BF16),
            pltpu.VMEM((2 * HALF, ROWS), BF16),
            pltpu.VMEM((ROWS, R), F32),
            pltpu.VMEM((2 * HALF, ROWS), BF16),
            pltpu.SemaphoreType.DMA((NB,)),
            pltpu.SemaphoreType.DMA((2 + ROWS // BR,)),
        ],
        compiler_params=params(),
        cost_estimate=cost(),
        name="tile_products",
    )(pos, cnt, place, in_hbm(blocks), in_hbm(left), in_hbm(right_test))


def gene_kernel(chunks, pieces, place, *refs):
    left, tile, mine, other, rows = refs[:pieces], refs[pieces], refs[-2 - chunks], refs[-1 - chunks : -1], refs[-1]
    halves = []
    for ref in left:
        halves += [ref.at[i : i + HALF] for i in range(0, ref.shape[0], HALF)]
    order_rows(place, halves, rows)
    for j in range(COLS // SPAN):
        cols = slice(j * SPAN, (j + 1) * SPAN)
        acc = jnp.dot(rows[...], tile[:, cols], preferred_element_type=F32)
        for c in range(chunks):
            at = 2 * HALF * c
            mine[c, :, cols] = acc[at : at + HALF]
            encode_part(acc[at + HALF : at + 2 * HALF], other[c], j)


def in_hbm(a):
    return pltpu.with_memory_space_constraint(a, pltpu.HBM)


def in_vmem(a):
    return pltpu.with_memory_space_constraint(a, pltpu.VMEM)


def gene(place, left, tile, through=(), after=()):
    height = sum(piece.shape[0] for piece in left)
    chunks = height // (2 * HALF)
    coded = jax.ShapeDtypeStruct((HALF, COLS + 128), I16)
    first_in = len(left) + 2
    return pl.pallas_call(
        functools.partial(gene_kernel, chunks, len(left)),
        out_shape=[jax.ShapeDtypeStruct(a.shape, a.dtype) for a in through] + [pltpu.VMEM((chunks, HALF, COLS), F32)] + [coded] * chunks,
        in_specs=[SMEM] + [VMEM] * (len(left) + 1) + [ANY] * (len(through) + len(after)),
        out_specs=[ANY] * len(through) + [VMEM] * (chunks + 1),
        scratch_shapes=[pltpu.VMEM((height, ROWS), BF16)],
        input_output_aliases={first_in + i: i for i in range(len(through))},
        compiler_params=params(),
        cost_estimate=cost(),
        name="gene_products",
    )(place, *left, tile, *through, *after)


def middle_kernel(place, right, low, high, to_next, to_prev, nearby, sems):
    gets = []
    for i, d in enumerate((1, 3)):
        at = pl.multiple_of(((place[1] + d) & 3) * 2 * BR, 2 * BR)
        gets.append(pltpu.make_async_copy(right.at[pl.ds(at, 2 * BR), :], nearby.at[i], sems.at[i]))
    for g in gets:
        g.start()
    gets[0].wait()
    to_next[:BR, :] = encode(nearby[0, :BR, :] + decode(low[...]))
    to_next[BR:, :] = encode(nearby[0, BR:, :])
    gets[1].wait()
    to_prev[:BR, :] = encode(nearby[1, :BR, :])
    to_prev[BR:, :] = encode(nearby[1, BR:, :] + decode(high[...]))


def middle(place, right, low, high):
    return pl.pallas_call(
        middle_kernel,
        out_shape=[jax.ShapeDtypeStruct((2 * BR, R + 128), I16)] * 2,
        in_specs=[SMEM, ANY, VMEM, VMEM],
        out_specs=[VMEM, VMEM],
        scratch_shapes=[pltpu.VMEM((2, 2 * BR, R), F32), pltpu.SemaphoreType.DMA((2,))],
        compiler_params=params(),
        cost_estimate=cost(10**10),
        name="right_middle",
    )(place, right, low, high)


def fold_rows_kernel(place, right, prev, following, after, keep, out1, out2, out3, own, sem):
    at = pl.multiple_of(place[1] * 2 * BR, 2 * BR)
    get = pltpu.make_async_copy(right.at[pl.ds(at, 2 * BR), :], own, sem)
    get.start()
    get.wait()
    for d, out in enumerate((keep, out1, out2, out3)):
        part = pl.ds(pl.multiple_of(((place[2] + d) & 3) * 128, 128), 128)
        total = own[part, :] + decode(prev[part, :]) + decode(following[part, :])
        out[...] = total if d == 0 else encode(total)


def fold_rows(place, right, prev, following, after):
    coded = jax.ShapeDtypeStruct((128, R + 128), I16)
    return pl.pallas_call(
        fold_rows_kernel,
        out_shape=[jax.ShapeDtypeStruct((128, R), F32), coded, coded, coded],
        in_specs=[SMEM, ANY, VMEM, VMEM, ANY],
        out_specs=[VMEM] * 4,
        scratch_shapes=[pltpu.VMEM((2 * BR, R), F32), pltpu.SemaphoreType.DMA],
        compiler_params=params(),
        cost_estimate=cost(10**9),
        name="right_fold",
    )(place, right, prev, following, after)


def sum_rows_kernel(keep, q1, q2, q3, out):
    out[...] = keep[...] + decode(q1[...]) + decode(q2[...]) + decode(q3[...])


def sum_rows(*parts):
    return pl.pallas_call(
        sum_rows_kernel,
        out_shape=jax.ShapeDtypeStruct((128, R), F32),
        in_specs=[VMEM] * 4,
        out_specs=VMEM,
        compiler_params=params(),
        cost_estimate=cost(),
        name="right_sum",
    )(*parts)


def pack_kernel(place, m0, mn, mf, r0, rn, rf, rp, keep, out1, out2, out3, total):
    total[0] = m0[0] + decode(r0[...])
    total[1] = mn[0] + decode(rn[...])
    total[2] = mf[0] + decode(rf[...])
    total[3] = mn[1] + decode(rp[...])
    keep[...] = total[place[3]]
    for d, out in ((1, out1), (2, out2), (3, out3)):
        out[...] = encode(total[(place[3] + d) & 3])


def pack(place, m0, mn, mf, *theirs):
    coded = jax.ShapeDtypeStruct((HALF, COLS + 128), I16)
    return pl.pallas_call(
        pack_kernel,
        out_shape=[pltpu.VMEM((HALF, COLS), F32), coded, coded, coded],
        in_specs=[SMEM] + [VMEM] * 7,
        out_specs=[VMEM] * 4,
        scratch_shapes=[pltpu.VMEM((4, HALF, COLS), F32)],
        compiler_params=params(),
        cost_estimate=cost(),
        name="pack_gene",
    )(place, in_vmem(m0), in_vmem(mn), in_vmem(mf), *theirs)


def finish_kernel(keep, q1, q2, q3, old, rt, after, sketch, coded, parts):
    total = keep[...] + decode(q1[...]) + decode(q2[...]) + decode(q3[...])
    sketch[...] = old[...] + total
    high = total.astype(BF16)
    parts[0:HALF, :] = high
    parts[HALF : 2 * HALF, :] = (total - high.astype(F32)).astype(BF16)
    product = jnp.dot(parts[...], rt[...], preferred_element_type=F32)
    coded[...] = encode(product[:HALF, :] + product[HALF:, :])


def finish(keep, q1, q2, q3, old, rt, after):
    return pl.pallas_call(
        finish_kernel,
        out_shape=[jax.ShapeDtypeStruct((HALF, COLS), F32), jax.ShapeDtypeStruct((HALF, R + 128), I16)],
        in_specs=[VMEM] * 6 + [ANY],
        out_specs=[VMEM] * 2,
        scratch_shapes=[pltpu.VMEM((2 * HALF, COLS), BF16)],
        compiler_params=params(),
        cost_estimate=cost(),
        name="gene_core",
    )(in_vmem(keep), q1, q2, q3, old, rt, after)


def fold_kernel(last, slot, q0, q1, q2, q3, out, terms):
    for d, q in enumerate((q0, q1, q2, q3)):
        terms[slot[d]] = decode(q[...])
    total = ((terms[0] + terms[1]) + terms[2]) + terms[3]
    out[...] = total if last else encode(total)


def fold(last, slot, *q):
    shape = jax.ShapeDtypeStruct((HALF, R), F32) if last else jax.ShapeDtypeStruct((HALF, R + 128), I16)
    return pl.pallas_call(
        functools.partial(fold_kernel, last),
        out_shape=shape,
        in_specs=[SMEM] + [VMEM] * 4,
        out_specs=VMEM,
        scratch_shapes=[pltpu.VMEM((4, HALF, R), F32)],
        compiler_params=params(),
        cost_estimate=cost(),
        name="fold_core",
    )(slot, *q)


def shift(n, d):
    return [(i, (i + d) % n) for i in range(n)]


def cell_shift(dz, dc):
    return [(z * 2 + c, ((z + dz) % 4) * 2 + (c + dc) % 2) for z in range(4) for c in range(2)]


def body(blocks, block_pos, block_count, test_right, test_left, gene_sketch_old):
    cell, y, x = lax.axis_index("cell"), lax.axis_index("gene"), lax.axis_index("rank")
    z, core = cell // 2, cell % 2
    place = jnp.stack([core, y, x, (z - x) % 4]).astype(jnp.int32)
    offsets = jnp.arange(4, dtype=jnp.int32)
    mate = lambda a: lax.ppermute(a, "cell", cell_shift(0, 1))
    move = lambda a, axis, d: lax.ppermute(a, axis, shift(4, d % 4))
    left = test_left.T
    from_prev, from_next = move(left, "rank", 1), move(left, "rank", -1)
    tile, right, far_low, far_high, m0, o0 = first(
        block_pos[0, 0], block_count[0, 0].reshape(1), place, blocks[0, 0], left, test_right
    )
    low, high = move(far_low, "gene", 1), move(far_high, "gene", -1)
    to_next, to_prev = middle(place, right, low, high)
    y_prev, y_next = move(to_next, "gene", 1), move(to_prev, "gene", -1)
    low_half, high_half, m0 = lax.optimization_barrier((from_prev[:HALF], from_next[HALF:], m0))
    left_low, left_high = move(low_half, "rank", 1), move(high_half, "rank", -1)
    mn, on, op = gene(place, [from_next, from_prev], tile)
    o0, on, op, mf, of = gene(place, [left_low, left_high], tile, [o0, on, op], [to_next])
    keep, s1, s2, s3 = pack(place, m0, mn, mf, mate(o0), mate(on), mate(of), mate(op))
    right_keep, *right_sent = fold_rows(place, right, y_prev, y_next, s1)
    right_got = [move(q, "rank", d) for d, q in zip((1, 2, 3), right_sent)]
    right_mine = sum_rows(right_keep, *right_got)
    along = lambda q, d: lax.ppermute(q, "cell", cell_shift(d, 0))
    gene_sketch, coded = finish(keep, along(s1, 1), along(s2, 2), along(s3, 3), gene_sketch_old, test_right, right_mine)
    over_y = [coded] + [move(coded, "gene", d) for d in (1, 2, 3)]
    coded = fold(False, (y - offsets) % 4, *over_y)
    over_x = [coded] + [move(coded, "rank", d) for d in (1, 2, 3)]
    core_sum = fold(True, (x - offsets) % 4, *over_x)
    return (right_mine, gene_sketch, core_sum)


def solution(mesh):
    return jax.shard_map(
        body,
        mesh=mesh,
        in_specs=(
            P("cell", ("gene", "rank"), None, None, None),
            P("cell", ("gene", "rank"), None),
            P("cell", ("gene", "rank")),
            P(("gene", "rank"), None),
            P("cell", "rank"),
            P("cell", ("gene", "rank")),
        ),
        out_specs=(P(("cell", "gene", "rank"), None), P("cell", ("gene", "rank")), P("cell", None)),
        check_vma=False,
    )
```

```python
import functools

import jax
import jax.numpy as jnp
from jax import lax
from jax.experimental import pallas as pl
from jax.experimental.pallas import tpu as pltpu
from jax.sharding import PartitionSpec as P

ROWS = 2048
COLS = 2048
BR, BC = 256, 128
NB = 96
R = 512
HALF = 96
SPAN = 512
LIMIT = 24 * 1024 * 1024
F32 = jnp.float32
BF16 = jnp.bfloat16
I16 = jnp.int16
ANY = pl.BlockSpec(memory_space=pl.ANY)
HBM = pl.BlockSpec(memory_space=pltpu.HBM)
VMEM = pl.BlockSpec(memory_space=pltpu.VMEM)
SMEM = pl.BlockSpec(memory_space=pltpu.SMEM)


def params(**kw):
    return pltpu.CompilerParams(vmem_limit_bytes=LIMIT, **kw)


def cost(flops=1):
    return pl.CostEstimate(flops=flops, bytes_accessed=1, transcendentals=0)


def encode(x):
    rows, cols = x.shape
    lane = lax.broadcasted_iota(jnp.int32, (rows, 128), 1)
    codes = jnp.zeros((rows, 128), jnp.int32)
    parts = []
    for j in range(cols // SPAN):
        part = x[:, j * SPAN : (j + 1) * SPAN]
        top = jnp.max(jnp.abs(part), axis=1, keepdims=True)
        code = jnp.ceil(jnp.log2(jnp.maximum(top, 1e-30) * (1.0 / 32760.0)) * 256.0)
        inverse = jnp.exp2(code * (-1.0 / 256.0))
        parts.append(jnp.round(part * inverse).astype(jnp.int32).astype(I16))
        codes = jnp.where(lane == j, code.astype(jnp.int32), codes)
    return jnp.concatenate(parts + [codes.astype(I16)], axis=1)


def encode_part(part, out, j):
    rows = part.shape[0]
    end = out.shape[1] - 128
    lane = lax.broadcasted_iota(jnp.int32, (rows, 128), 1)
    coded = encode(part)
    out[:, j * SPAN : (j + 1) * SPAN] = coded[:, :SPAN]
    codes = coded[:, SPAN:].astype(jnp.int32)
    if j == 0:
        out[:, end:] = codes.astype(I16)
    else:
        moved = jnp.where(lane == j, codes[:, 0:1], out[:, end:].astype(jnp.int32))
        out[:, end:] = moved.astype(I16)


def decode(q):
    rows, cols = q.shape
    cols -= 128
    scales = jnp.exp2(q[:, cols:].astype(jnp.int32).astype(F32) * (1.0 / 256.0))
    parts = []
    for j in range(cols // SPAN):
        parts.append(q[:, j * SPAN : (j + 1) * SPAN].astype(jnp.int32).astype(F32) * scales[:, j : j + 1])
    return jnp.concatenate(parts, axis=1)


def first_kernel(pos, cnt, place, blocks, left_test, right_test, tile, right_out, far_low, far_high, mine, other, rt, left, right, rows, sems, io):
    live = cnt[0]
    get_rt = pltpu.make_async_copy(right_test, rt, io.at[0])
    get_rt.start()
    get_left = pltpu.make_async_copy(left_test, left, io.at[1 + ROWS // BR])
    get_left.start()

    def clear(i, _):
        tile[pl.ds(pl.multiple_of(i * 64, 64), 64), :] = jnp.zeros((64, COLS), BF16)

    lax.fori_loop(0, ROWS // 64, clear, None)

    def copy_of(s):
        p = pos[s]
        row = pl.multiple_of((p >> 4) * BR, BR)
        col = pl.multiple_of((p & 15) * BC, BC)
        return pltpu.make_async_copy(blocks.at[s], tile.at[pl.ds(row, BR), pl.ds(col, BC)], sems.at[s])

    lax.fori_loop(0, live, lambda s, _: copy_of(s).start(), None)
    get_left.wait()
    order_rows(place, [left.at[0:HALF], left.at[HALF : 2 * HALF]], rows)
    get_rt.wait()
    lax.fori_loop(0, live, lambda s, _: copy_of(s).wait(), None)

    def put_of(i):
        rows = pl.ds(pl.multiple_of(i * BR, BR), BR)
        return pltpu.make_async_copy(right.at[rows, :], right_out.at[rows, :], io.at[1 + i])

    def multiply(i, _):
        rows = pl.ds(pl.multiple_of(i * BR, BR), BR)
        right[rows, :] = jnp.dot(tile[rows, :], rt[...], preferred_element_type=F32)
        put_of(i).start()

    lax.fori_loop(0, ROWS // BR, multiply, None)
    far = pl.multiple_of(((place[1] + 2) & 3) * 2 * BR, 2 * BR)
    far_low[...] = encode(right[pl.ds(far, BR), :])
    far_high[...] = encode(right[pl.ds(far + BR, BR), :])
    for j in range(COLS // SPAN):
        cols = slice(j * SPAN, (j + 1) * SPAN)
        acc = jnp.dot(rows[...], tile[:, cols], preferred_element_type=F32)
        mine[0, :, cols] = acc[:HALF]
        encode_part(acc[HALF:], other, j)
    lax.fori_loop(0, ROWS // BR, lambda i, _: put_of(i).wait(), None)


def order_rows(place, halves, rows):
    for c in range(len(halves) // 2):
        low, high = halves[2 * c], halves[2 * c + 1]
        at = 2 * HALF * c

        @pl.when(place[0] == 0)
        def _():
            rows[at : at + HALF, :] = low[...]
            rows[at + HALF : at + 2 * HALF, :] = high[...]

        @pl.when(place[0] == 1)
        def _():
            rows[at : at + HALF, :] = high[...]
            rows[at + HALF : at + 2 * HALF, :] = low[...]


def first(pos, cnt, place, blocks, left, right_test):
    return pl.pallas_call(
        first_kernel,
        out_shape=[
            pltpu.VMEM((ROWS, COLS), BF16),
            jax.ShapeDtypeStruct((ROWS, R), F32),
            jax.ShapeDtypeStruct((BR, R + 128), I16),
            jax.ShapeDtypeStruct((BR, R + 128), I16),
            pltpu.VMEM((1, HALF, COLS), F32),
            jax.ShapeDtypeStruct((HALF, COLS + 128), I16),
        ],
        in_specs=[SMEM, SMEM, SMEM, HBM, HBM, HBM],
        out_specs=[VMEM, HBM, VMEM, VMEM, VMEM, VMEM],
        scratch_shapes=[
            pltpu.VMEM((COLS, R), BF16),
            pltpu.VMEM((2 * HALF, ROWS), BF16),
            pltpu.VMEM((ROWS, R), F32),
            pltpu.VMEM((2 * HALF, ROWS), BF16),
            pltpu.SemaphoreType.DMA((NB,)),
            pltpu.SemaphoreType.DMA((2 + ROWS // BR,)),
        ],
        compiler_params=params(),
        cost_estimate=cost(),
        name="tile_products",
    )(pos, cnt, place, in_hbm(blocks), in_hbm(left), in_hbm(right_test))


def gene_kernel(chunks, pieces, place, *refs):
    left, tile, (mine, other, rows) = refs[:pieces], refs[pieces], refs[-3:]
    halves = []
    for ref in left:
        halves += [ref.at[i : i + HALF] for i in range(0, ref.shape[0], HALF)]
    order_rows(place, halves, rows)
    for j in range(COLS // SPAN):
        cols = slice(j * SPAN, (j + 1) * SPAN)
        acc = jnp.dot(rows[...], tile[:, cols], preferred_element_type=F32)
        for c in range(chunks):
            at = 2 * HALF * c
            mine[c, :, cols] = acc[at : at + HALF]
            encode_part(acc[at + HALF : at + 2 * HALF], other.at[c * HALF : (c + 1) * HALF], j)


def in_hbm(a):
    return pltpu.with_memory_space_constraint(a, pltpu.HBM)


def in_vmem(a):
    return pltpu.with_memory_space_constraint(a, pltpu.VMEM)


def gene(place, left, tile, through=(), after=()):
    height = sum(piece.shape[0] for piece in left)
    chunks = height // (2 * HALF)
    coded = jax.ShapeDtypeStruct((chunks * HALF, COLS + 128), I16)
    first_in = len(left) + 2
    return pl.pallas_call(
        functools.partial(gene_kernel, chunks, len(left)),
        out_shape=[jax.ShapeDtypeStruct(a.shape, a.dtype) for a in through] + [pltpu.VMEM((chunks, HALF, COLS), F32), coded],
        in_specs=[SMEM] + [VMEM] * (len(left) + 1) + [ANY] * (len(through) + len(after)),
        out_specs=[ANY] * len(through) + [VMEM] * 2,
        scratch_shapes=[pltpu.VMEM((height, ROWS), BF16)],
        input_output_aliases={first_in + i: i for i in range(len(through))},
        compiler_params=params(),
        cost_estimate=cost(),
        name="gene_products",
    )(place, *left, tile, *through, *after)


def middle_kernel(place, right, low, high, to_next, to_prev, nearby, sems):
    gets = []
    for i, d in enumerate((1, 3)):
        at = pl.multiple_of(((place[1] + d) & 3) * 2 * BR, 2 * BR)
        gets.append(pltpu.make_async_copy(right.at[pl.ds(at, 2 * BR), :], nearby.at[i], sems.at[i]))
    for g in gets:
        g.start()
    gets[0].wait()
    to_next[:BR, :] = encode(nearby[0, :BR, :] + decode(low[...]))
    to_next[BR:, :] = encode(nearby[0, BR:, :])
    gets[1].wait()
    to_prev[:BR, :] = encode(nearby[1, :BR, :])
    to_prev[BR:, :] = encode(nearby[1, BR:, :] + decode(high[...]))


def middle(place, right, low, high):
    return pl.pallas_call(
        middle_kernel,
        out_shape=[jax.ShapeDtypeStruct((2 * BR, R + 128), I16)] * 2,
        in_specs=[SMEM, ANY, VMEM, VMEM],
        out_specs=[VMEM, VMEM],
        scratch_shapes=[pltpu.VMEM((2, 2 * BR, R), F32), pltpu.SemaphoreType.DMA((2,))],
        compiler_params=params(),
        cost_estimate=cost(10**10),
        name="right_middle",
    )(place, right, low, high)


def fold_rows_kernel(place, right, prev, following, after, keep, out1, out2, out3, own, sem):
    at = pl.multiple_of(place[1] * 2 * BR, 2 * BR)
    get = pltpu.make_async_copy(right.at[pl.ds(at, 2 * BR), :], own, sem)
    get.start()
    get.wait()
    for d, out in enumerate((keep, out1, out2, out3)):
        part = pl.ds(pl.multiple_of(((place[2] + d) & 3) * 128, 128), 128)
        total = own[part, :] + decode(prev[part, :]) + decode(following[part, :])
        out[...] = total if d == 0 else encode(total)


def fold_rows(place, right, prev, following, after):
    coded = jax.ShapeDtypeStruct((128, R + 128), I16)
    return pl.pallas_call(
        fold_rows_kernel,
        out_shape=[jax.ShapeDtypeStruct((128, R), F32), coded, coded, coded],
        in_specs=[SMEM, ANY, VMEM, VMEM, ANY],
        out_specs=[VMEM] * 4,
        scratch_shapes=[pltpu.VMEM((2 * BR, R), F32), pltpu.SemaphoreType.DMA],
        compiler_params=params(),
        cost_estimate=cost(1 * 10**9),
        name="right_fold",
    )(place, right, prev, following, after)


def sum_rows_kernel(keep, q1, q2, q3, out, token):
    token[...] = keep[0:8, 0:128]
    out[...] = keep[...] + decode(q1[...]) + decode(q2[...]) + decode(q3[...])


def sum_rows(*parts):
    return pl.pallas_call(
        sum_rows_kernel,
        out_shape=[jax.ShapeDtypeStruct((128, R), F32), pltpu.VMEM((8, 128), F32)],
        in_specs=[VMEM] * 4,
        out_specs=[VMEM, VMEM],
        compiler_params=params(),
        cost_estimate=cost(0 * 10**9),
        name="right_sum",
    )(*parts)


def pack_kernel(place, m0, mn, mf, r0, rn, rf, keep, out1, out2, out3, total):
    total[0] = m0[0] + decode(r0[...])
    total[1] = mn[0] + decode(rn[0:HALF, :])
    total[2] = mf[0] + decode(rf[...])
    total[3] = mn[1] + decode(rn[HALF : 2 * HALF, :])
    keep[...] = total[place[3]]
    for d, out in ((1, out1), (2, out2), (3, out3)):
        out[...] = encode(total[(place[3] + d) & 3])


def pack(place, m0, mn, mf, *theirs):
    coded = jax.ShapeDtypeStruct((HALF, COLS + 128), I16)
    return pl.pallas_call(
        pack_kernel,
        out_shape=[pltpu.VMEM((HALF, COLS), F32), coded, coded, coded],
        in_specs=[SMEM] + [VMEM] * 6,
        out_specs=[VMEM] * 4,
        scratch_shapes=[pltpu.VMEM((4, HALF, COLS), F32)],
        compiler_params=params(),
        cost_estimate=cost(),
        name="pack_gene",
    )(place, in_vmem(m0), in_vmem(mn), in_vmem(mf), *theirs)


def finish_kernel(keep, q1, q2, q3, old, rt, after, sketch, coded, parts):
    total = keep[...] + decode(q1[...]) + decode(q2[...]) + decode(q3[...])
    sketch[...] = old[...] + total
    high = total.astype(BF16)
    parts[0:HALF, :] = high
    parts[HALF : 2 * HALF, :] = (total - high.astype(F32)).astype(BF16)
    product = jnp.dot(parts[...], rt[...], preferred_element_type=F32)
    coded[...] = encode(product[:HALF, :] + product[HALF:, :])


def finish(keep, q1, q2, q3, old, rt, after):
    return pl.pallas_call(
        finish_kernel,
        out_shape=[jax.ShapeDtypeStruct((HALF, COLS), F32), jax.ShapeDtypeStruct((HALF, R + 128), I16)],
        in_specs=[VMEM] * 6 + [ANY],
        out_specs=[VMEM] * 2,
        scratch_shapes=[pltpu.VMEM((2 * HALF, COLS), BF16)],
        compiler_params=params(),
        cost_estimate=cost(),
        name="gene_core",
    )(in_vmem(keep), q1, q2, q3, old, rt, after)


def fold_kernel(last, slot, q0, q1, q2, q3, *refs):
    out, terms = refs[-2:]
    for d, q in enumerate((q0, q1, q2, q3)):
        terms[slot[d]] = decode(q[...])
    total = ((terms[0] + terms[1]) + terms[2]) + terms[3]
    out[...] = total if last else encode(total)


def fold(last, slot, q, after=()):
    shape = jax.ShapeDtypeStruct((HALF, R), F32) if last else jax.ShapeDtypeStruct((HALF, R + 128), I16)
    return pl.pallas_call(
        functools.partial(fold_kernel, last),
        out_shape=shape,
        in_specs=[SMEM] + [VMEM] * (4 + len(after)),
        out_specs=VMEM,
        scratch_shapes=[pltpu.VMEM((4, HALF, R), F32)],
        compiler_params=params(),
        cost_estimate=cost(),
        name="fold_core",
    )(slot, *q, *after)


def shift(n, d):
    return [(i, (i + d) % n) for i in range(n)]


def cell_shift(dz, dc):
    return [(z * 2 + c, ((z + dz) % 4) * 2 + (c + dc) % 2) for z in range(4) for c in range(2)]


def body(blocks, block_pos, block_count, test_right, test_left, gene_sketch_old):
    cell, y, x = lax.axis_index("cell"), lax.axis_index("gene"), lax.axis_index("rank")
    z, core = cell // 2, cell % 2
    place = jnp.stack([core, y, x, (z - x) % 4]).astype(jnp.int32)
    offsets = jnp.arange(4, dtype=jnp.int32)
    mate = lambda a: lax.ppermute(a, "cell", cell_shift(0, 1))
    move = lambda a, axis, d: lax.ppermute(a, axis, shift(4, d % 4))
    left = test_left.T
    from_prev, from_next = move(left, "rank", 1), move(left, "rank", -1)
    tile, right, far_low, far_high, m0, o0 = first(
        block_pos[0, 0], block_count[0, 0].reshape(1), place, blocks[0, 0], left, test_right
    )
    low, high = move(far_low, "gene", 1), move(far_high, "gene", -1)
    to_next, to_prev = middle(place, right, low, high)
    y_prev, y_next = move(to_next, "gene", 1), move(to_prev, "gene", -1)
    low_half, high_half, m0 = lax.optimization_barrier((from_prev[:HALF], from_next[HALF:], m0))
    left_low, left_high = move(low_half, "rank", 1), move(high_half, "rank", -1)
    mn, on = gene(place, [from_next, from_prev], tile)
    mf, of = gene(place, [left_low, left_high], tile, [], [to_next])
    keep, s1, s2, s3 = pack(place, m0, mn, mf, mate(o0), mate(on), mate(of))
    right_keep, *right_sent = fold_rows(place, right, y_prev, y_next, s1)
    right_got = [move(q, "rank", d) for d, q in zip((1, 2, 3), right_sent)]
    right_mine, token = sum_rows(right_keep, *right_got)
    along = lambda q, d: lax.ppermute(q, "cell", cell_shift(d, 0))
    gene_sketch, coded = finish(keep, along(s1, 1), along(s2, 2), along(s3, 3), gene_sketch_old, test_right, right_sent[0])
    over_y = [coded] + [move(coded, "gene", d) for d in (1, 2, 3)]
    coded = fold(False, (y - offsets) % 4, over_y, [in_vmem(token)])
    over_x = [coded] + [move(coded, "rank", d) for d in (1, 2, 3)]
    core_sum = fold(True, (x - offsets) % 4, over_x)
    return (right_mine, gene_sketch, core_sum)


def solution(mesh):
    return jax.shard_map(
        body,
        mesh=mesh,
        in_specs=(
            P("cell", ("gene", "rank"), None, None, None),
            P("cell", ("gene", "rank"), None),
            P("cell", ("gene", "rank")),
            P(("gene", "rank"), None),
            P("cell", "rank"),
            P("cell", ("gene", "rank")),
        ),
        out_specs=(P(("cell", "gene", "rank"), None), P("cell", ("gene", "rank")), P("cell", None)),
        check_vma=False,
    )
```

```python
import functools

import jax
import jax.numpy as jnp
from jax import lax
from jax.experimental import pallas as pl
from jax.experimental.pallas import tpu as pltpu
from jax.sharding import PartitionSpec as P

ROWS = 2048
COLS = 2048
BR, BC = 256, 128
NB = 96
R = 512
HALF = 96
SPAN = 512
LIMIT = 24 * 1024 * 1024
F32 = jnp.float32
BF16 = jnp.bfloat16
I16 = jnp.int16
ANY = pl.BlockSpec(memory_space=pl.ANY)
HBM = pl.BlockSpec(memory_space=pltpu.HBM)
VMEM = pl.BlockSpec(memory_space=pltpu.VMEM)
SMEM = pl.BlockSpec(memory_space=pltpu.SMEM)


def params(**kw):
    return pltpu.CompilerParams(vmem_limit_bytes=LIMIT, **kw)


def cost(flops=1):
    return pl.CostEstimate(flops=flops, bytes_accessed=1, transcendentals=0)


def encode(x):
    rows, cols = x.shape
    lane = lax.broadcasted_iota(jnp.int32, (rows, 128), 1)
    codes = jnp.zeros((rows, 128), jnp.int32)
    parts = []
    for j in range(cols // SPAN):
        part = x[:, j * SPAN : (j + 1) * SPAN]
        top = jnp.max(jnp.abs(part), axis=1, keepdims=True)
        code = jnp.ceil(jnp.log2(jnp.maximum(top, 1e-30) * (1.0 / 32760.0)) * 256.0)
        inverse = jnp.exp2(code * (-1.0 / 256.0))
        parts.append(jnp.round(part * inverse).astype(jnp.int32).astype(I16))
        codes = jnp.where(lane == j, code.astype(jnp.int32), codes)
    return jnp.concatenate(parts + [codes.astype(I16)], axis=1)


def encode_part(part, out, j):
    rows = part.shape[0]
    end = out.shape[1] - 128
    lane = lax.broadcasted_iota(jnp.int32, (rows, 128), 1)
    coded = encode(part)
    out[:, j * SPAN : (j + 1) * SPAN] = coded[:, :SPAN]
    codes = coded[:, SPAN:].astype(jnp.int32)
    if j == 0:
        out[:, end:] = codes.astype(I16)
    else:
        moved = jnp.where(lane == j, codes[:, 0:1], out[:, end:].astype(jnp.int32))
        out[:, end:] = moved.astype(I16)


def decode(q):
    rows, cols = q.shape
    cols -= 128
    scales = jnp.exp2(q[:, cols:].astype(jnp.int32).astype(F32) * (1.0 / 256.0))
    parts = []
    for j in range(cols // SPAN):
        parts.append(q[:, j * SPAN : (j + 1) * SPAN].astype(jnp.int32).astype(F32) * scales[:, j : j + 1])
    return jnp.concatenate(parts, axis=1)


def first_kernel(pos, cnt, place, blocks, left_test, right_test, tile, right_out, far_low, far_high, mine, other, rt, left, right, rows, sems, io):
    live = cnt[0]
    get_rt = pltpu.make_async_copy(right_test, rt, io.at[0])
    get_rt.start()
    get_left = pltpu.make_async_copy(left_test, left, io.at[1 + ROWS // BR])
    get_left.start()

    def clear(i, _):
        tile[pl.ds(pl.multiple_of(i * 64, 64), 64), :] = jnp.zeros((64, COLS), BF16)

    lax.fori_loop(0, ROWS // 64, clear, None)

    def copy_of(s):
        p = pos[s]
        row = pl.multiple_of((p >> 4) * BR, BR)
        col = pl.multiple_of((p & 15) * BC, BC)
        return pltpu.make_async_copy(blocks.at[s], tile.at[pl.ds(row, BR), pl.ds(col, BC)], sems.at[s])

    lax.fori_loop(0, live, lambda s, _: copy_of(s).start(), None)
    get_left.wait()
    order_rows(place, [left.at[0:HALF], left.at[HALF : 2 * HALF]], rows)
    get_rt.wait()
    lax.fori_loop(0, live, lambda s, _: copy_of(s).wait(), None)

    def put_of(i):
        rows = pl.ds(pl.multiple_of(i * BR, BR), BR)
        return pltpu.make_async_copy(right.at[rows, :], right_out.at[rows, :], io.at[1 + i])

    def multiply(i, _):
        rows = pl.ds(pl.multiple_of(i * BR, BR), BR)
        right[rows, :] = jnp.dot(tile[rows, :], rt[...], preferred_element_type=F32)
        put_of(i).start()

    lax.fori_loop(0, ROWS // BR, multiply, None)
    far = pl.multiple_of(((place[1] + 2) & 3) * 2 * BR, 2 * BR)
    far_low[...] = encode(right[pl.ds(far, BR), :])
    far_high[...] = encode(right[pl.ds(far + BR, BR), :])
    for j in range(COLS // SPAN):
        cols = slice(j * SPAN, (j + 1) * SPAN)
        acc = jnp.dot(rows[...], tile[:, cols], preferred_element_type=F32)
        mine[0, :, cols] = acc[:HALF]
        encode_part(acc[HALF:], other, j)
    lax.fori_loop(0, ROWS // BR, lambda i, _: put_of(i).wait(), None)


def order_rows(place, halves, rows):
    for c in range(len(halves) // 2):
        low, high = halves[2 * c], halves[2 * c + 1]
        at = 2 * HALF * c

        @pl.when(place[0] == 0)
        def _():
            rows[at : at + HALF, :] = low[...]
            rows[at + HALF : at + 2 * HALF, :] = high[...]

        @pl.when(place[0] == 1)
        def _():
            rows[at : at + HALF, :] = high[...]
            rows[at + HALF : at + 2 * HALF, :] = low[...]


def first(pos, cnt, place, blocks, left, right_test):
    return pl.pallas_call(
        first_kernel,
        out_shape=[
            pltpu.VMEM((ROWS, COLS), BF16),
            jax.ShapeDtypeStruct((ROWS, R), F32),
            jax.ShapeDtypeStruct((BR, R + 128), I16),
            jax.ShapeDtypeStruct((BR, R + 128), I16),
            pltpu.VMEM((1, HALF, COLS), F32),
            jax.ShapeDtypeStruct((HALF, COLS + 128), I16),
        ],
        in_specs=[SMEM, SMEM, SMEM, HBM, HBM, HBM],
        out_specs=[VMEM, HBM, VMEM, VMEM, VMEM, VMEM],
        scratch_shapes=[
            pltpu.VMEM((COLS, R), BF16),
            pltpu.VMEM((2 * HALF, ROWS), BF16),
            pltpu.VMEM((ROWS, R), F32),
            pltpu.VMEM((2 * HALF, ROWS), BF16),
            pltpu.SemaphoreType.DMA((NB,)),
            pltpu.SemaphoreType.DMA((2 + ROWS // BR,)),
        ],
        compiler_params=params(),
        cost_estimate=cost(),
        name="tile_products",
    )(pos, cnt, place, in_hbm(blocks), in_hbm(left), in_hbm(right_test))


def gene_kernel(chunks, pieces, place, *refs):
    left, tile, (mine, other, rows) = refs[:pieces], refs[pieces], refs[-3:]
    halves = []
    for ref in left:
        halves += [ref.at[i : i + HALF] for i in range(0, ref.shape[0], HALF)]
    order_rows(place, halves, rows)
    for j in range(COLS // SPAN):
        cols = slice(j * SPAN, (j + 1) * SPAN)
        acc = jnp.dot(rows[...], tile[:, cols], preferred_element_type=F32)
        for c in range(chunks):
            at = 2 * HALF * c
            mine[c, :, cols] = acc[at : at + HALF]
            encode_part(acc[at + HALF : at + 2 * HALF], other.at[c * HALF : (c + 1) * HALF], j)


def in_hbm(a):
    return pltpu.with_memory_space_constraint(a, pltpu.HBM)


def in_vmem(a):
    return pltpu.with_memory_space_constraint(a, pltpu.VMEM)


def gene(place, left, tile, through=(), after=()):
    height = sum(piece.shape[0] for piece in left)
    chunks = height // (2 * HALF)
    coded = jax.ShapeDtypeStruct((chunks * HALF, COLS + 128), I16)
    first_in = len(left) + 2
    return pl.pallas_call(
        functools.partial(gene_kernel, chunks, len(left)),
        out_shape=[jax.ShapeDtypeStruct(a.shape, a.dtype) for a in through] + [pltpu.VMEM((chunks, HALF, COLS), F32), coded],
        in_specs=[SMEM] + [VMEM] * (len(left) + 1) + [ANY] * (len(through) + len(after)),
        out_specs=[ANY] * len(through) + [VMEM] * 2,
        scratch_shapes=[pltpu.VMEM((height, ROWS), BF16)],
        input_output_aliases={first_in + i: i for i in range(len(through))},
        compiler_params=params(),
        cost_estimate=cost(),
        name="gene_products",
    )(place, *left, tile, *through, *after)


def middle_kernel(place, right, low, high, to_next, to_prev, nearby, sems):
    gets = []
    for i, d in enumerate((1, 3)):
        at = pl.multiple_of(((place[1] + d) & 3) * 2 * BR, 2 * BR)
        gets.append(pltpu.make_async_copy(right.at[pl.ds(at, 2 * BR), :], nearby.at[i], sems.at[i]))
    for g in gets:
        g.start()
    gets[0].wait()
    to_next[:BR, :] = encode(nearby[0, :BR, :] + decode(low[...]))
    to_next[BR:, :] = encode(nearby[0, BR:, :])
    gets[1].wait()
    to_prev[:BR, :] = encode(nearby[1, :BR, :])
    to_prev[BR:, :] = encode(nearby[1, BR:, :] + decode(high[...]))


def middle(place, right, low, high):
    return pl.pallas_call(
        middle_kernel,
        out_shape=[jax.ShapeDtypeStruct((2 * BR, R + 128), I16)] * 2,
        in_specs=[SMEM, ANY, VMEM, VMEM],
        out_specs=[VMEM, VMEM],
        scratch_shapes=[pltpu.VMEM((2, 2 * BR, R), F32), pltpu.SemaphoreType.DMA((2,))],
        compiler_params=params(),
        cost_estimate=cost(10**10),
        name="right_middle",
    )(place, right, low, high)


def fold_rows_kernel(place, right, prev, following, after, keep, out1, out2, out3, own, sem):
    at = pl.multiple_of(place[1] * 2 * BR, 2 * BR)
    get = pltpu.make_async_copy(right.at[pl.ds(at, 2 * BR), :], own, sem)
    get.start()
    get.wait()
    for d, out in enumerate((keep, out1, out2, out3)):
        part = pl.ds(pl.multiple_of(((place[2] + d) & 3) * 128, 128), 128)
        total = own[part, :] + decode(prev[part, :]) + decode(following[part, :])
        out[...] = total if d == 0 else encode(total)


def fold_rows(place, right, prev, following, after):
    coded = jax.ShapeDtypeStruct((128, R + 128), I16)
    return pl.pallas_call(
        fold_rows_kernel,
        out_shape=[jax.ShapeDtypeStruct((128, R), F32), coded, coded, coded],
        in_specs=[SMEM, ANY, VMEM, VMEM, ANY],
        out_specs=[VMEM] * 4,
        scratch_shapes=[pltpu.VMEM((2 * BR, R), F32), pltpu.SemaphoreType.DMA],
        compiler_params=params(),
        cost_estimate=cost(1 * 10**9),
        name="right_fold",
    )(place, right, prev, following, after)


def sum_rows_kernel(keep, q1, q2, q3, out, token):
    token[...] = keep[0:8, 0:128]
    out[...] = keep[...] + decode(q1[...]) + decode(q2[...]) + decode(q3[...])


def sum_rows(*parts):
    return pl.pallas_call(
        sum_rows_kernel,
        out_shape=[jax.ShapeDtypeStruct((128, R), F32), pltpu.VMEM((8, 128), F32)],
        in_specs=[VMEM] * 4,
        out_specs=[VMEM, VMEM],
        compiler_params=params(),
        cost_estimate=cost(0 * 10**9),
        name="right_sum",
    )(*parts)


def core_kernel(place, m0, mn, mf, r0, rn, rf, rt, total, keep, out1, out2, out3, parts, terms):
    total[0] = m0[0] + decode(r0[...])
    total[1] = mn[0] + decode(rn[0:HALF, :])
    total[2] = mf[0] + decode(rf[...])
    total[3] = mn[1] + decode(rn[HALF : 2 * HALF, :])
    for i in range(4):
        high = total[i].astype(BF16)
        parts[2 * i * HALF : (2 * i + 1) * HALF, :] = high
        parts[(2 * i + 1) * HALF : (2 * i + 2) * HALF, :] = (total[i] - high.astype(F32)).astype(BF16)
    product = jnp.dot(parts[...], rt[...], preferred_element_type=F32)
    for i in range(4):
        terms[i] = product[2 * i * HALF : (2 * i + 1) * HALF, :] + product[(2 * i + 1) * HALF : (2 * i + 2) * HALF, :]
    keep[...] = terms[place[3]]
    for d, out in ((1, out1), (2, out2), (3, out3)):
        out[...] = encode(terms[(place[3] + d) & 3])


def core_share(place, m0, mn, mf, *theirs):
    coded = jax.ShapeDtypeStruct((HALF, R + 128), I16)
    return pl.pallas_call(
        core_kernel,
        out_shape=[pltpu.VMEM((4, HALF, COLS), F32), pltpu.VMEM((HALF, R), F32), coded, coded, coded],
        in_specs=[SMEM] + [VMEM] * 7,
        out_specs=[VMEM] * 5,
        scratch_shapes=[pltpu.VMEM((8 * HALF, COLS), BF16), pltpu.VMEM((4, HALF, R), F32)],
        compiler_params=params(),
        cost_estimate=cost(),
        name="core_share",
    )(place, in_vmem(m0), in_vmem(mn), in_vmem(mf), *theirs)


def pack_kernel(place, total, keep, out1, out2, out3):
    keep[...] = total[place[3]]
    for d, out in ((1, out1), (2, out2), (3, out3)):
        out[...] = encode(total[(place[3] + d) & 3])


def pack(place, total):
    coded = jax.ShapeDtypeStruct((HALF, COLS + 128), I16)
    return pl.pallas_call(
        pack_kernel,
        out_shape=[pltpu.VMEM((HALF, COLS), F32), coded, coded, coded],
        in_specs=[SMEM, VMEM],
        out_specs=[VMEM] * 4,
        compiler_params=params(),
        cost_estimate=cost(),
        name="pack_gene",
    )(place, in_vmem(total))


def finish_kernel(keep, q1, q2, q3, old, after, sketch):
    sketch[...] = old[...] + (keep[...] + decode(q1[...]) + decode(q2[...]) + decode(q3[...]))


def finish(keep, q1, q2, q3, old, after):
    return pl.pallas_call(
        finish_kernel,
        out_shape=jax.ShapeDtypeStruct((HALF, COLS), F32),
        in_specs=[VMEM] * 6,
        out_specs=VMEM,
        compiler_params=params(),
        cost_estimate=cost(),
        name="gene_sum",
    )(in_vmem(keep), q1, q2, q3, old, after)


def gather_core_kernel(keep, q1, q2, q3, out):
    out[...] = encode(keep[...] + decode(q1[...]) + decode(q2[...]) + decode(q3[...]))


def gather_core(keep, *q):
    return pl.pallas_call(
        gather_core_kernel,
        out_shape=jax.ShapeDtypeStruct((HALF, R + 128), I16),
        in_specs=[VMEM] * 4,
        out_specs=VMEM,
        compiler_params=params(),
        cost_estimate=cost(),
        name="core_cells",
    )(in_vmem(keep), *q)


def fold_kernel(last, slot, q0, q1, q2, q3, *refs):
    out, terms = refs[-3] if last else refs[-2], refs[-1]
    if last:
        refs[-2][...] = jnp.zeros((8, 128), F32)
    for d, q in enumerate((q0, q1, q2, q3)):
        terms[slot[d]] = decode(q[...])
    total = ((terms[0] + terms[1]) + terms[2]) + terms[3]
    out[...] = total if last else encode(total)


def fold(last, slot, q, after=()):
    shape = jax.ShapeDtypeStruct((HALF, R), F32) if last else jax.ShapeDtypeStruct((HALF, R + 128), I16)
    return pl.pallas_call(
        functools.partial(fold_kernel, last),
        out_shape=[shape, pltpu.VMEM((8, 128), F32)] if last else shape,
        in_specs=[SMEM] + [VMEM] * (4 + len(after)),
        out_specs=[VMEM, VMEM] if last else VMEM,
        scratch_shapes=[pltpu.VMEM((4, HALF, R), F32)],
        compiler_params=params(),
        cost_estimate=cost(),
        name="fold_core",
    )(slot, *q, *after)


def shift(n, d):
    return [(i, (i + d) % n) for i in range(n)]


def cell_shift(dz, dc):
    return [(z * 2 + c, ((z + dz) % 4) * 2 + (c + dc) % 2) for z in range(4) for c in range(2)]


def body(blocks, block_pos, block_count, test_right, test_left, gene_sketch_old):
    cell, y, x = lax.axis_index("cell"), lax.axis_index("gene"), lax.axis_index("rank")
    z, core = cell // 2, cell % 2
    place = jnp.stack([core, y, x, (z - x) % 4]).astype(jnp.int32)
    offsets = jnp.arange(4, dtype=jnp.int32)
    mate = lambda a: lax.ppermute(a, "cell", cell_shift(0, 1))
    move = lambda a, axis, d: lax.ppermute(a, axis, shift(4, d % 4))
    left = test_left.T
    from_prev, from_next = move(left, "rank", 1), move(left, "rank", -1)
    tile, right, far_low, far_high, m0, o0 = first(
        block_pos[0, 0], block_count[0, 0].reshape(1), place, blocks[0, 0], left, test_right
    )
    low, high = move(far_low, "gene", 1), move(far_high, "gene", -1)
    to_next, to_prev = middle(place, right, low, high)
    y_prev, y_next = move(to_next, "gene", 1), move(to_prev, "gene", -1)
    low_half, high_half, m0 = lax.optimization_barrier((from_prev[:HALF], from_next[HALF:], m0))
    left_low, left_high = move(low_half, "rank", 1), move(high_half, "rank", -1)
    mn, on = gene(place, [from_next, from_prev], tile)
    mf, of = gene(place, [left_low, left_high], tile, [], [to_next])
    total, core_keep, p1, p2, p3 = core_share(place, m0, mn, mf, mate(o0), mate(on), mate(of), test_right)
    keep, s1, s2, s3 = pack(place, total)
    right_keep, *right_sent = fold_rows(place, right, y_prev, y_next, s1)
    right_got = [move(q, "rank", d) for d, q in zip((1, 2, 3), right_sent)]
    right_mine, token = sum_rows(right_keep, *right_got)
    along = lambda q, d: lax.ppermute(q, "cell", cell_shift(d, 0))
    coded = gather_core(core_keep, along(p1, 1), along(p2, 2), along(p3, 3))
    over_y = [coded] + [move(coded, "gene", d) for d in (1, 2, 3)]
    coded = fold(False, (y - offsets) % 4, over_y)
    over_x = [coded] + [move(coded, "rank", d) for d in (1, 2, 3)]
    core_sum, mark = fold(True, (x - offsets) % 4, over_x, [in_vmem(token)])
    gene_sketch = finish(keep, along(s1, 1), along(s2, 2), along(s3, 3), gene_sketch_old, in_vmem(mark))
    return (right_mine, gene_sketch, core_sum)


def solution(mesh):
    return jax.shard_map(
        body,
        mesh=mesh,
        in_specs=(
            P("cell", ("gene", "rank"), None, None, None),
            P("cell", ("gene", "rank"), None),
            P("cell", ("gene", "rank")),
            P(("gene", "rank"), None),
            P("cell", "rank"),
            P("cell", ("gene", "rank")),
        ),
        out_specs=(P(("cell", "gene", "rank"), None), P("cell", ("gene", "rank")), P("cell", None)),
        check_vma=False,
    )
```

```python
import functools

import jax
import jax.numpy as jnp
from jax import lax
from jax.experimental import pallas as pl
from jax.experimental.pallas import tpu as pltpu
from jax.sharding import PartitionSpec as P

ROWS = 2048
COLS = 2048
BR, BC = 256, 128
NB = 96
R = 512
HALF = 96
SPAN = 512
LIMIT = 24 * 1024 * 1024
F32 = jnp.float32
BF16 = jnp.bfloat16
I16 = jnp.int16
ANY = pl.BlockSpec(memory_space=pl.ANY)
HBM = pl.BlockSpec(memory_space=pltpu.HBM)
VMEM = pl.BlockSpec(memory_space=pltpu.VMEM)
SMEM = pl.BlockSpec(memory_space=pltpu.SMEM)


def params(**kw):
    return pltpu.CompilerParams(vmem_limit_bytes=LIMIT, **kw)


def cost(flops=1):
    return pl.CostEstimate(flops=flops, bytes_accessed=1, transcendentals=0)


def encode(x):
    rows, cols = x.shape
    lane = lax.broadcasted_iota(jnp.int32, (rows, 128), 1)
    codes = jnp.zeros((rows, 128), jnp.int32)
    parts = []
    for j in range(cols // SPAN):
        part = x[:, j * SPAN : (j + 1) * SPAN]
        top = jnp.max(jnp.abs(part), axis=1, keepdims=True)
        code = jnp.ceil(jnp.log2(jnp.maximum(top, 1e-30) * (1.0 / 32760.0)) * 256.0)
        inverse = jnp.exp2(code * (-1.0 / 256.0))
        parts.append(jnp.round(part * inverse).astype(jnp.int32).astype(I16))
        codes = jnp.where(lane == j, code.astype(jnp.int32), codes)
    return jnp.concatenate(parts + [codes.astype(I16)], axis=1)


def encode_part(part, out, j):
    rows = part.shape[0]
    end = out.shape[1] - 128
    lane = lax.broadcasted_iota(jnp.int32, (rows, 128), 1)
    coded = encode(part)
    out[:, j * SPAN : (j + 1) * SPAN] = coded[:, :SPAN]
    codes = coded[:, SPAN:].astype(jnp.int32)
    if j == 0:
        out[:, end:] = codes.astype(I16)
    else:
        moved = jnp.where(lane == j, codes[:, 0:1], out[:, end:].astype(jnp.int32))
        out[:, end:] = moved.astype(I16)


def decode(q):
    rows, cols = q.shape
    cols -= 128
    scales = jnp.exp2(q[:, cols:].astype(jnp.int32).astype(F32) * (1.0 / 256.0))
    parts = []
    for j in range(cols // SPAN):
        parts.append(q[:, j * SPAN : (j + 1) * SPAN].astype(jnp.int32).astype(F32) * scales[:, j : j + 1])
    return jnp.concatenate(parts, axis=1)


def first_kernel(pos, cnt, place, blocks, left_test, right_test, tile, right_out, far_low, far_high, mine, other, rt, left, right, rows, sems, io):
    live = cnt[0]
    get_rt = pltpu.make_async_copy(right_test, rt, io.at[0])
    get_rt.start()
    get_left = pltpu.make_async_copy(left_test, left, io.at[1 + ROWS // BR])
    get_left.start()

    def clear(i, _):
        tile[pl.ds(pl.multiple_of(i * 64, 64), 64), :] = jnp.zeros((64, COLS), BF16)

    lax.fori_loop(0, ROWS // 64, clear, None)

    def copy_of(s):
        p = pos[s]
        row = pl.multiple_of((p >> 4) * BR, BR)
        col = pl.multiple_of((p & 15) * BC, BC)
        return pltpu.make_async_copy(blocks.at[s], tile.at[pl.ds(row, BR), pl.ds(col, BC)], sems.at[s])

    lax.fori_loop(0, live, lambda s, _: copy_of(s).start(), None)
    get_left.wait()
    order_rows(place, [left.at[0:HALF], left.at[HALF : 2 * HALF]], rows)
    get_rt.wait()
    lax.fori_loop(0, live, lambda s, _: copy_of(s).wait(), None)

    def put_of(i):
        rows = pl.ds(pl.multiple_of(i * BR, BR), BR)
        return pltpu.make_async_copy(right.at[rows, :], right_out.at[rows, :], io.at[1 + i])

    def multiply(i, _):
        rows = pl.ds(pl.multiple_of(i * BR, BR), BR)
        right[rows, :] = jnp.dot(tile[rows, :], rt[...], preferred_element_type=F32)
        put_of(i).start()

    lax.fori_loop(0, ROWS // BR, multiply, None)
    far = pl.multiple_of(((place[1] + 2) & 3) * 2 * BR, 2 * BR)
    far_low[...] = encode(right[pl.ds(far, BR), :])
    far_high[...] = encode(right[pl.ds(far + BR, BR), :])
    for j in range(COLS // SPAN):
        cols = slice(j * SPAN, (j + 1) * SPAN)
        acc = jnp.dot(rows[...], tile[:, cols], preferred_element_type=F32)
        mine[0, :, cols] = acc[:HALF]
        encode_part(acc[HALF:], other, j)
    lax.fori_loop(0, ROWS // BR, lambda i, _: put_of(i).wait(), None)


def order_rows(place, halves, rows):
    for c in range(len(halves) // 2):
        low, high = halves[2 * c], halves[2 * c + 1]
        at = 2 * HALF * c

        @pl.when(place[0] == 0)
        def _():
            rows[at : at + HALF, :] = low[...]
            rows[at + HALF : at + 2 * HALF, :] = high[...]

        @pl.when(place[0] == 1)
        def _():
            rows[at : at + HALF, :] = high[...]
            rows[at + HALF : at + 2 * HALF, :] = low[...]


def first(pos, cnt, place, blocks, left, right_test):
    return pl.pallas_call(
        first_kernel,
        out_shape=[
            pltpu.VMEM((ROWS, COLS), BF16),
            jax.ShapeDtypeStruct((ROWS, R), F32),
            jax.ShapeDtypeStruct((BR, R + 128), I16),
            jax.ShapeDtypeStruct((BR, R + 128), I16),
            pltpu.VMEM((1, HALF, COLS), F32),
            jax.ShapeDtypeStruct((HALF, COLS + 128), I16),
        ],
        in_specs=[SMEM, SMEM, SMEM, HBM, HBM, HBM],
        out_specs=[VMEM, HBM, VMEM, VMEM, VMEM, VMEM],
        scratch_shapes=[
            pltpu.VMEM((COLS, R), BF16),
            pltpu.VMEM((2 * HALF, ROWS), BF16),
            pltpu.VMEM((ROWS, R), F32),
            pltpu.VMEM((2 * HALF, ROWS), BF16),
            pltpu.SemaphoreType.DMA((NB,)),
            pltpu.SemaphoreType.DMA((2 + ROWS // BR,)),
        ],
        compiler_params=params(),
        cost_estimate=cost(),
        name="tile_products",
    )(pos, cnt, place, in_hbm(blocks), in_hbm(left), in_hbm(right_test))


def gene_kernel(chunks, pieces, place, *refs):
    left, tile, (mine, other, rows) = refs[:pieces], refs[pieces], refs[-3:]
    halves = []
    for ref in left:
        halves += [ref.at[i : i + HALF] for i in range(0, ref.shape[0], HALF)]
    order_rows(place, halves, rows)
    for j in range(COLS // SPAN):
        cols = slice(j * SPAN, (j + 1) * SPAN)
        acc = jnp.dot(rows[...], tile[:, cols], preferred_element_type=F32)
        for c in range(chunks):
            at = 2 * HALF * c
            mine[c, :, cols] = acc[at : at + HALF]
            encode_part(acc[at + HALF : at + 2 * HALF], other.at[c * HALF : (c + 1) * HALF], j)


def in_hbm(a):
    return pltpu.with_memory_space_constraint(a, pltpu.HBM)


def in_vmem(a):
    return pltpu.with_memory_space_constraint(a, pltpu.VMEM)


def gene(place, left, tile, through=(), after=()):
    height = sum(piece.shape[0] for piece in left)
    chunks = height // (2 * HALF)
    coded = jax.ShapeDtypeStruct((chunks * HALF, COLS + 128), I16)
    first_in = len(left) + 2
    return pl.pallas_call(
        functools.partial(gene_kernel, chunks, len(left)),
        out_shape=[jax.ShapeDtypeStruct(a.shape, a.dtype) for a in through] + [pltpu.VMEM((chunks, HALF, COLS), F32), coded],
        in_specs=[SMEM] + [VMEM] * (len(left) + 1) + [ANY] * (len(through) + len(after)),
        out_specs=[ANY] * len(through) + [VMEM] * 2,
        scratch_shapes=[pltpu.VMEM((height, ROWS), BF16)],
        input_output_aliases={first_in + i: i for i in range(len(through))},
        compiler_params=params(),
        cost_estimate=cost(),
        name="gene_products",
    )(place, *left, tile, *through, *after)


def middle_kernel(place, right, low, high, to_next, to_prev, nearby, sems):
    gets = []
    for i, d in enumerate((1, 3)):
        at = pl.multiple_of(((place[1] + d) & 3) * 2 * BR, 2 * BR)
        gets.append(pltpu.make_async_copy(right.at[pl.ds(at, 2 * BR), :], nearby.at[i], sems.at[i]))
    for g in gets:
        g.start()
    gets[0].wait()
    to_next[:BR, :] = encode(nearby[0, :BR, :] + decode(low[...]))
    to_next[BR:, :] = encode(nearby[0, BR:, :])
    gets[1].wait()
    to_prev[:BR, :] = encode(nearby[1, :BR, :])
    to_prev[BR:, :] = encode(nearby[1, BR:, :] + decode(high[...]))


def middle(place, right, low, high):
    return pl.pallas_call(
        middle_kernel,
        out_shape=[jax.ShapeDtypeStruct((2 * BR, R + 128), I16)] * 2,
        in_specs=[SMEM, ANY, VMEM, VMEM],
        out_specs=[VMEM, VMEM],
        scratch_shapes=[pltpu.VMEM((2, 2 * BR, R), F32), pltpu.SemaphoreType.DMA((2,))],
        compiler_params=params(),
        cost_estimate=cost(10**10),
        name="right_middle",
    )(place, right, low, high)


def fold_rows_kernel(place, right, prev, following, after, keep, out1, out2, out3, own, sem):
    at = pl.multiple_of(place[1] * 2 * BR, 2 * BR)
    get = pltpu.make_async_copy(right.at[pl.ds(at, 2 * BR), :], own, sem)
    get.start()
    get.wait()
    for d, out in enumerate((keep, out1, out2, out3)):
        part = pl.ds(pl.multiple_of(((place[2] + d) & 3) * 128, 128), 128)
        total = own[part, :] + decode(prev[part, :]) + decode(following[part, :])
        out[...] = total if d == 0 else encode(total)


def fold_rows(place, right, prev, following, after):
    coded = jax.ShapeDtypeStruct((128, R + 128), I16)
    return pl.pallas_call(
        fold_rows_kernel,
        out_shape=[jax.ShapeDtypeStruct((128, R), F32), coded, coded, coded],
        in_specs=[SMEM, ANY, VMEM, VMEM, ANY],
        out_specs=[VMEM] * 4,
        scratch_shapes=[pltpu.VMEM((2 * BR, R), F32), pltpu.SemaphoreType.DMA],
        compiler_params=params(),
        cost_estimate=cost(1 * 10**9),
        name="right_fold",
    )(place, right, prev, following, after)


def sum_rows_kernel(keep, q1, q2, q3, out, token):
    token[...] = keep[0:8, 0:128]
    out[...] = keep[...] + decode(q1[...]) + decode(q2[...]) + decode(q3[...])


def sum_rows(*parts):
    return pl.pallas_call(
        sum_rows_kernel,
        out_shape=[jax.ShapeDtypeStruct((128, R), F32), pltpu.VMEM((8, 128), F32)],
        in_specs=[VMEM] * 4,
        out_specs=[VMEM, VMEM],
        compiler_params=params(),
        cost_estimate=cost(0 * 10**9),
        name="right_sum",
    )(*parts)


def core_kernel(place, m0, mn, mf, r0, rn, rf, rt, total, keep, out1, out2, out3, parts, terms):
    total[0] = m0[0] + decode(r0[...])
    total[1] = mn[0] + decode(rn[0:HALF, :])
    total[2] = mf[0] + decode(rf[...])
    total[3] = mn[1] + decode(rn[HALF : 2 * HALF, :])
    for i in range(4):
        high = total[i].astype(BF16)
        parts[2 * i * HALF : (2 * i + 1) * HALF, :] = high
        parts[(2 * i + 1) * HALF : (2 * i + 2) * HALF, :] = (total[i] - high.astype(F32)).astype(BF16)
    product = jnp.dot(parts[...], rt[...], preferred_element_type=F32)
    for i in range(4):
        terms[i] = product[2 * i * HALF : (2 * i + 1) * HALF, :] + product[(2 * i + 1) * HALF : (2 * i + 2) * HALF, :]
    keep[...] = terms[place[3]]
    for d, out in ((1, out1), (2, out2), (3, out3)):
        out[...] = encode(terms[(place[3] + d) & 3])


def core_share(place, m0, mn, mf, *theirs):
    coded = jax.ShapeDtypeStruct((HALF, R + 128), I16)
    return pl.pallas_call(
        core_kernel,
        out_shape=[pltpu.VMEM((4, HALF, COLS), F32), pltpu.VMEM((HALF, R), F32), coded, coded, coded],
        in_specs=[SMEM] + [VMEM] * 7,
        out_specs=[VMEM] * 5,
        scratch_shapes=[pltpu.VMEM((8 * HALF, COLS), BF16), pltpu.VMEM((4, HALF, R), F32)],
        compiler_params=params(),
        cost_estimate=cost(),
        name="core_share",
    )(place, in_vmem(m0), in_vmem(mn), in_vmem(mf), *theirs)


def pack_kernel(place, total, keep, out1, out2, out3):
    keep[...] = total[place[3]]
    for d, out in ((1, out1), (2, out2), (3, out3)):
        out[...] = encode(total[(place[3] + d) & 3])


def pack(place, total):
    coded = jax.ShapeDtypeStruct((HALF, COLS + 128), I16)
    return pl.pallas_call(
        pack_kernel,
        out_shape=[pltpu.VMEM((HALF, COLS), F32), coded, coded, coded],
        in_specs=[SMEM, VMEM],
        out_specs=[VMEM] * 4,
        compiler_params=params(),
        cost_estimate=cost(),
        name="pack_gene",
    )(place, in_vmem(total))


def finish_kernel(keep, q1, q2, q3, old, after, sketch):
    sketch[...] = old[...] + (keep[...] + decode(q1[...]) + decode(q2[...]) + decode(q3[...]))


def finish(keep, q1, q2, q3, old, after):
    return pl.pallas_call(
        finish_kernel,
        out_shape=jax.ShapeDtypeStruct((HALF, COLS), F32),
        in_specs=[VMEM] * 6,
        out_specs=VMEM,
        compiler_params=params(),
        cost_estimate=cost(),
        name="gene_sum",
    )(in_vmem(keep), q1, q2, q3, old, after)


def gather_core_kernel(keep, q1, q2, q3, out):
    out[...] = encode(keep[...] + decode(q1[...]) + decode(q2[...]) + decode(q3[...]))


def gather_core(keep, *q):
    return pl.pallas_call(
        gather_core_kernel,
        out_shape=jax.ShapeDtypeStruct((HALF, R + 128), I16),
        in_specs=[VMEM] * 4,
        out_specs=VMEM,
        compiler_params=params(),
        cost_estimate=cost(),
        name="core_cells",
    )(in_vmem(keep), *q)


def fold_kernel(last, slot, q0, q1, q2, q3, *refs):
    out, terms = refs[-3] if last else refs[-2], refs[-1]
    if last:
        refs[-2][...] = jnp.zeros((8, 128), F32)
    for d, q in enumerate((q0, q1, q2, q3)):
        terms[slot[d]] = decode(q[...])
    total = ((terms[0] + terms[1]) + terms[2]) + terms[3]
    out[...] = total if last else encode(total)


def fold(last, slot, q, after=()):
    shape = pltpu.VMEM((HALF, R), F32) if last else jax.ShapeDtypeStruct((HALF, R + 128), I16)
    return pl.pallas_call(
        functools.partial(fold_kernel, last),
        out_shape=[shape, pltpu.VMEM((8, 128), F32)] if last else shape,
        in_specs=[SMEM] + [VMEM] * (4 + len(after)),
        out_specs=[VMEM, VMEM] if last else VMEM,
        scratch_shapes=[pltpu.VMEM((4, HALF, R), F32)],
        compiler_params=params(),
        cost_estimate=cost(),
        name="fold_core",
    )(slot, *q, *after)


def shift(n, d):
    return [(i, (i + d) % n) for i in range(n)]


def cell_shift(dz, dc):
    return [(z * 2 + c, ((z + dz) % 4) * 2 + (c + dc) % 2) for z in range(4) for c in range(2)]


def body(blocks, block_pos, block_count, test_right, test_left, gene_sketch_old):
    cell, y, x = lax.axis_index("cell"), lax.axis_index("gene"), lax.axis_index("rank")
    z, core = cell // 2, cell % 2
    place = jnp.stack([core, y, x, (z - x) % 4]).astype(jnp.int32)
    offsets = jnp.arange(4, dtype=jnp.int32)
    mate = lambda a: lax.ppermute(a, "cell", cell_shift(0, 1))
    move = lambda a, axis, d: lax.ppermute(a, axis, shift(4, d % 4))
    left = test_left.T
    from_next = move(left, "rank", -1)
    from_prev = move(left, "rank", 1)
    tile, right, far_low, far_high, m0, o0 = first(
        block_pos[0, 0], block_count[0, 0].reshape(1), place, blocks[0, 0], left, test_right
    )
    low, high = move(far_low, "gene", 1), move(far_high, "gene", -1)
    to_next, to_prev = middle(place, right, low, high)
    y_prev, y_next = move(to_next, "gene", 1), move(to_prev, "gene", -1)
    low_half, high_half, m0 = lax.optimization_barrier((from_prev[:HALF], from_next[HALF:], m0))
    left_low, left_high = move(low_half, "rank", 1), move(high_half, "rank", -1)
    mn, on = gene(place, [from_next, from_prev], tile)
    mf, of = gene(place, [left_low, left_high], tile, [], [to_next])
    total, core_keep, p1, p2, p3 = core_share(place, m0, mn, mf, mate(o0), mate(on), mate(of), test_right)
    keep, s1, s2, s3 = pack(place, total)
    right_keep, *right_sent = fold_rows(place, right, y_prev, y_next, s1)
    right_got = [move(q, "rank", d) for d, q in zip((1, 2, 3), right_sent)]
    right_mine, token = sum_rows(right_keep, *right_got)
    along = lambda q, d: lax.ppermute(q, "cell", cell_shift(d, 0))
    coded = gather_core(core_keep, along(p1, 1), along(p2, 2), along(p3, 3))
    over_y = [coded] + [move(coded, "gene", d) for d in (1, 2, 3)]
    coded = fold(False, (y - offsets) % 4, over_y)
    over_x = [coded] + [move(coded, "rank", d) for d in (1, 2, 3)]
    core_sum, mark = fold(True, (x - offsets) % 4, over_x, [in_vmem(token)])
    gene_sketch = finish(keep, along(s1, 1), along(s2, 2), along(s3, 3), gene_sketch_old, in_vmem(mark))
    return (right_mine, gene_sketch, core_sum)


def solution(mesh):
    return jax.shard_map(
        body,
        mesh=mesh,
        in_specs=(
            P("cell", ("gene", "rank"), None, None, None),
            P("cell", ("gene", "rank"), None),
            P("cell", ("gene", "rank")),
            P(("gene", "rank"), None),
            P("cell", "rank"),
            P("cell", ("gene", "rank")),
        ),
        out_specs=(P(("cell", "gene", "rank"), None), P("cell", ("gene", "rank")), P("cell", None)),
        check_vma=False,
    )
```
